32 devices in a mesh: row: 16 (over z, x, core), rep: 2 (over y).
Axes of the slice: x: 2, y: 2, z: 4, core: 2. Of those that a mesh axis runs over, the one named last changes fastest.
Arguments:
- features: bfloat16 [32768, 256], P('row'), may hold values from -6 to 6
- adjacency: bfloat16 [256, 48, 128, 128], P('row', 'rep'), may hold values from 0 to 3, as said below
- columns: int32 [256, 48], P('row', 'rep'), may hold values from 0 to 255, as said below
- live: int32 [256], P('row'), may hold values from 0 to 48, as said below
- w_self: bfloat16 [256, 256], replicated, may hold values from -0.375 to 0.375
- w_neigh: bfloat16 [256, 256], replicated, may hold values from -4 to 4
- bias: float32 [256], replicated, may hold values from -3 to 3
Outputs:
- mixed: bfloat16 [32768, 256], P(('row', 'rep'))
The draws below stay inside these ranges and needn't reach their ends.
Inputs may be any that keep to these rules, and one draw needn't show every extreme that they name: `adjacency`: edge weights are nonnegative; most entries are zero, and some nodes have no edges at all. `columns`: the column block of every slot of block row b lies in the block rows held by a row index at most 2 away from the one holding b (never outside the graph). Slots at or after live[b] are ignored; some block row uses all 48 slots.
All inputs are finite; a program needn't handle non-finite values.
Results may differ from the reference program's by a relative error of at most 0.0048.
Values may be sent and summed in bfloat16 or wider, within the bound.
No kernel may reach another device: no remote copies, remote signals or barrier semaphores. Data moves between devices by JAX's collectives and lax.ppermute only.
A program may use at most 64 MiB of HBM per device.

```python
import math
import jax
import jax.numpy as jnp
from jax import lax

F = 256
BLOCK = 128
NB_DEV = 16
K = 48
REACH = 2
NBLK = 256
NODES = 32768


def draw_adjacency(key, part):
    first_key, second_key = jax.random.split(key, 2)
    uniform_draw = jax.random.uniform(first_key, (NBLK, K, BLOCK, BLOCK), jnp.float32)
    present = uniform_draw < 0.025
    scaled = uniform_draw / 0.025
    keep_rows = jax.random.randint(second_key, (NBLK, 1, BLOCK, 1), 0, 64) > 0
    weights = 0.1 * jnp.exp(scaled * math.log(30.0))
    weights = jnp.minimum(weights, 3.0)
    return jnp.where(present & keep_rows, weights, 0.0).astype(jnp.bfloat16)


def draw_columns(key, part):
    first_key, second_key = jax.random.split(key, 2)
    device_count = NBLK // NB_DEV
    block_ids = jnp.arange(NBLK, dtype=jnp.int32)[:, None]
    holder = block_ids // NB_DEV
    jumps = jax.random.randint(first_key, (NBLK, K), -REACH, REACH + 1)
    target = jnp.clip(holder + jumps, 0, device_count - 1)
    inside = jax.random.randint(second_key, (NBLK, K), 0, NB_DEV)
    return (target * NB_DEV + inside).astype(jnp.int32)


def draw_live(key, part):
    first_key, second_key, third_key = jax.random.split(key, 3)
    device_count = NBLK // NB_DEV
    levels = jax.random.randint(first_key, (device_count,), 0, 4)
    capacity = jnp.maximum(K // jnp.left_shift(1, levels), 1)
    capacity_rows = jnp.repeat(capacity, NB_DEV)
    spread_bits = jax.random.randint(second_key, (NBLK,), 0, 1 << 20)
    lowest = capacity_rows // 2
    counts = lowest + spread_bits % (capacity_rows - lowest + 1)
    full_row = jax.random.randint(third_key, (), 0, NBLK)
    return jnp.where(jnp.arange(NBLK, dtype=jnp.int32) == full_row, K, counts).astype(jnp.int32)


def level_of(rng, dims, cuts, low, top_value):
    def one(position, shards_of):
        draws = jax.random.uniform(jax.random.fold_in(jax.random.fold_in(rng, 6), position), (shards_of,), jnp.float32, low / len(cuts), top_value / len(cuts))
        return jnp.repeat(jnp.exp(draws), dims[position] // shards_of).reshape((-1,) + (1,) * (len(dims) - position - 1))

    gain = one(*cuts[0])
    for cut in cuts[1:]:
        gain = gain * one(*cut)
    return gain


def gaussian(rng, extent, scale, most, shards=(), kind=jnp.bfloat16):
    drawn = jax.random.normal(rng, extent, jnp.float32) * scale
    if len(shards) > 0:
        drawn = level_of(rng, extent, shards, -0.22, 0.18) * drawn
    return jnp.clip(drawn, min=-most, max=most).astype(kind)


def setup_inputs(seed: int = 0) -> dict:
    splits = jax.random.split(jax.random.key(seed), 8)
    features = gaussian(splits[0], (NODES, F), 1.0, 6.0, ((0, 16),))
    adjacency = draw_adjacency(jax.random.fold_in(splits[7], 71), 0)
    columns = draw_columns(jax.random.fold_in(splits[7], 71), 0)
    live = draw_live(jax.random.fold_in(splits[7], 71), 0)
    w_self = gaussian(splits[4], (F, F), F ** -0.5, 0.375)
    w_neigh = gaussian(splits[5], (F, F), 1.0, 4.0)
    bias = gaussian(splits[6], (F,), 0.5, 3.0, (), jnp.float32)
    return {"features": features, "adjacency": adjacency, "columns": columns, "live": live, "w_self": w_self, "w_neigh": w_neigh, "bias": bias}


def reference(features, adjacency, columns, live, w_self, w_neigh, bias):
    feature_blocks = features.reshape(NBLK, BLOCK, F)
    slot_ids = jnp.arange(K, dtype=jnp.int32)

    def one_row(row_item):
        row_tiles, row_columns, row_count = row_item
        live_slots = slot_ids < row_count
        masked = jnp.where(live_slots[:, None, None], row_tiles.astype(jnp.float32), jnp.float32(0.0))
        source = feature_blocks[row_columns.astype(jnp.int32)].astype(jnp.float32)
        running = jnp.einsum("sij,sjf->if", masked, source)
        degree = jnp.sum(masked, axis=(0, 2))
        return running, degree

    totals, degrees = lax.map(one_row, (adjacency, columns, live))
    totals = totals.reshape(NODES, F)
    degrees = degrees.reshape(NODES)
    neighbor_mean = (totals / jnp.maximum(degrees, jnp.float32(1.0))[:, None]).astype(jnp.bfloat16)
    summed = jnp.dot(features, w_self, preferred_element_type=jnp.float32)
    summed = summed + jnp.dot(neighbor_mean, w_neigh, preferred_element_type=jnp.float32) + bias
    return jax.nn.relu(summed).astype(jnp.bfloat16)
```

```python
import functools

import jax
import jax.numpy as jnp
from jax import lax
from jax.experimental import pallas as pl
from jax.experimental.pallas import tpu as pltpu
from jax.sharding import PartitionSpec as P

OWN, PAIR, CROSS, AHEAD, LAST = range(5)
SOURCES = 5
HALVES = 2
CUTS = ((1,), (1,))
OVER_CUTS = (2, 1)
GROUP = 2
VMEM_BYTES = 6 << 20
TINY = pl.CostEstimate(flops=0, bytes_accessed=0, transcendentals=0)


def after(x, *others):
    return lax.optimization_barrier((x, *others))[0]


def in_hbm(x):
    return pltpu.with_memory_space_constraint(x, pltpu.HBM)


def in_vmem(x):
    return pltpu.with_memory_space_constraint(x, pltpu.VMEM)


def piece_starts(h, rows):
    return [rows * sum(CUTS[h][:q]) // sum(CUTS[h]) for q in range(len(CUTS[h]) + 1)]


def swap_route(count, bit):
    return [(i, i ^ bit) for i in range(count)]


def ahead_route(count):
    return [(i, (i + 4) % count if i % 4 < 2 else (i - 4) % count) for i in range(count)]


def degree_kernel(own_part, usable, place, adj, degree, tiles, sems):
    rows = degree.shape[0]
    first = (place[0] if own_part else 1 - place[0]) * rows
    loads = [pltpu.make_async_copy(adj.at[first + i], tiles.at[i], sems.at[i]) for i in range(rows)]
    for load in loads:
        load.start()
    for i in range(rows):
        loads[i].wait()
        degree[i : i + 1, :] = degree_row(tiles, i, usable[first + i])


def degree_row(tiles, i, count):
    slots, edge = tiles.shape[1], tiles.shape[2]
    acc = jnp.zeros((edge, edge), jnp.float32)
    for s in range(slots):
        t = tiles[i, s]
        acc = acc + jnp.where(s < count, t, jnp.zeros_like(t)).astype(jnp.float32)
    return jnp.sum(acc.T, axis=0, keepdims=True)


def token_kernel(value, out):
    out[...] = jnp.full(out.shape, value[0], out.dtype)


def base_kernel(place, feats, w_self, bias, base, own, sem):
    half = own.shape[0]
    copy = pltpu.make_async_copy(feats.at[pl.ds(pl.multiple_of(place[0] * half, half), half)], own, sem)
    copy.start()
    copy.wait()
    base[...] = jnp.dot(own[...], w_self[...], preferred_element_type=jnp.float32) + bias[...]


def product_kernel(own_part, halves, resident, index, place, adj, feats, pair, *rest):
    counts = [2 + 2 * OVER_CUTS[h] for h in halves]
    pieces, rest = rest[: sum(counts)], rest[sum(counts) :]
    outs, rest = rest[: len(halves)], rest[len(halves) :]
    if resident:
        tiles = adj
        window, window_sems = rest
    else:
        tiles, window, window_sems, tile_sems = rest
    rows, slots, edge = tiles.shape[0], tiles.shape[1], tiles.shape[2]
    part = window.shape[2]
    shard = 2 * rows * edge
    first = (place[0] if own_part else 1 - place[0]) * rows

    copies, by_cross, by_ahead = [], [], []
    for k, h in enumerate(halves):

        def move(ref, at, m):
            return pltpu.make_async_copy(ref, window.at[k, pl.ds(at, ref.shape[0])], window_sems.at[k, m])

        columns = pl.ds(h * part, part)
        at, n = sum(counts[:k]), OVER_CUTS[h]
        cross, ahead = pieces[at : at + 2]
        cross_over, ahead_over = pieces[at + 2 : at + 2 + n], pieces[at + 2 + n : at + 2 + 2 * n]
        copies += [move(feats.at[:, columns], OWN * shard, 0), move(pair.at[:, columns], PAIR * shard, 1)]
        copies += [move(cross, CROSS * shard, 2), move(ahead, AHEAD * shard, 3)]
        for q in range(n):
            by_cross.append(move(cross_over[q], LAST * shard + q * (shard // n), 4 + q))
            by_ahead.append(move(ahead_over[q], LAST * shard + q * (shard // n), 4 + q))
    for copy in copies:
        copy.start()

    @pl.when(place[1] == 1)
    def _():
        for copy in by_cross:
            copy.start()

    @pl.when(place[1] == 0)
    def _():
        for copy in by_ahead:
            copy.start()

    if not resident:
        loads = [pltpu.make_async_copy(adj.at[first + i], tiles.at[i], tile_sems.at[i]) for i in range(rows)]
        for load in loads:
            load.start()
    for k in range(len(halves)):
        window[k, pl.ds(SOURCES * shard, edge), :] = jnp.zeros((edge, part), window.dtype)
    for copy in copies + by_cross:
        copy.wait()

    def block(at):
        cut = pl.ds(pl.multiple_of(at * edge, edge), edge)
        return jnp.concatenate([window[k, cut, :] for k in range(len(halves))], axis=1)

    for g in range(0, rows, GROUP):
        if not resident:
            for i in range(g, g + GROUP):
                loads[i].wait()
        for i in range(g, g + GROUP):
            acc = None
            for s in range(0, slots, 2):
                left = jnp.concatenate([tiles[i, s], tiles[i, s + 1]], axis=1)
                right = jnp.concatenate([block(index[first + i, s]), block(index[first + i, s + 1])], axis=0)
                d = jnp.dot(left, right, preferred_element_type=jnp.float32)
                acc = d if acc is None else acc + d
            for k, out in enumerate(outs):
                out[i * edge : (i + 1) * edge, :] = acc[:, k * part : (k + 1) * part].astype(out.dtype)


def final_kernel(degree, degree_far, base, own0, far0, own1, far1, w_neigh, out):
    rows, edge = degree.shape
    for i in range(rows):
        total = degree[i : i + 1, :] + degree_far[i : i + 1, :]
        scale = 1.0 / jnp.maximum(total, 1.0)
        column = jnp.broadcast_to(scale, (edge, edge)).T
        cut = pl.ds(i * edge, edge)
        mean = jnp.concatenate(
            [
                ((own0[cut, :] + far0[cut, :].astype(jnp.float32)) * column).astype(jnp.bfloat16),
                ((own1[cut, :] + far1[cut, :].astype(jnp.float32)) * column).astype(jnp.bfloat16),
            ],
            axis=1,
        )
        mixed = base[cut, :] + jnp.dot(mean, w_neigh[...], preferred_element_type=jnp.float32)
        out[cut, :] = jnp.maximum(mixed, 0.0).astype(out.dtype)


def local(features, adjacency, columns, live, w_self, w_neigh, bias):
    rows, width = features.shape
    block_rows, slots, edge, _ = adjacency.shape
    count = lax.axis_size("row")
    place = lax.axis_index("row")
    replica = lax.axis_index("rep")
    part = width // HALVES
    out_rows = rows // 2

    usable = jnp.clip(live - replica * slots, 0, slots)
    spot = jnp.reshape(replica, (1,)).astype(jnp.int32)

    offset = columns // block_rows - place
    to_pair = 1 - 2 * (place % 2)
    to_cross = jnp.where(place % 4 < 2, 2, -2)
    source = jnp.where(offset == to_pair, PAIR, jnp.where(offset == -to_pair, LAST, OWN))
    source = jnp.where(offset == to_cross, CROSS, jnp.where(offset == -to_cross, AHEAD, source))
    index = source * block_rows + columns % block_rows
    dead = jnp.arange(slots, dtype=jnp.int32)[None, :] >= usable[:, None]
    index = jnp.where(dead, SOURCES * block_rows, index).astype(jnp.int32)

    smem = pl.BlockSpec(memory_space=pltpu.SMEM)
    vmem = pl.BlockSpec(memory_space=pltpu.VMEM)
    hbm = pl.BlockSpec(memory_space=pltpu.HBM)
    params = pltpu.CompilerParams(vmem_limit_bytes=VMEM_BYTES)

    def cross_of(h, q):
        starts = piece_starts(h, rows)
        sent = features[starts[q] : starts[q + 1], h * part : (h + 1) * part]
        return lax.ppermute(sent, "row", swap_route(count, 2))

    cross = [[cross_of(h, q) for q in range(len(CUTS[h]))] for h in range(HALVES)]
    pair = lax.ppermute(features, "row", swap_route(count, 1))

    wide = pltpu.CompilerParams(vmem_limit_bytes=16 << 20)
    anyw = pl.BlockSpec(memory_space=pl.ANY)
    adjacency = in_hbm(adjacency)

    def ahead_of(p):
        return lax.ppermute(p, "row", ahead_route(count))

    def over(p):
        return lax.ppermute(p, "row", swap_route(count, 1))

    held = (block_rows // 2, slots, edge, edge)
    sems = pltpu.SemaphoreType.DMA((block_rows // 2,))

    def degree_of(own_part, usable):
        shape = jax.ShapeDtypeStruct((block_rows // 2, edge), jnp.float32)
        tiles = pltpu.VMEM(held, jnp.bfloat16)
        outs = pl.pallas_call(
            functools.partial(degree_kernel, own_part),
            out_shape=[shape] if own_part else [shape, tiles],
            in_specs=[smem, smem, hbm],
            out_specs=[vmem] if own_part else [vmem, vmem],
            scratch_shapes=[tiles, sems] if own_part else [sems],
            compiler_params=wide if own_part else params,
            cost_estimate=TINY,
        )(usable, spot, adjacency)
        return outs[0] if own_part else (outs[0], in_vmem(outs[1]))

    def product_of(own_part, halves, tiles, *args, resident=False):
        kind = jnp.float32 if own_part else jnp.bfloat16
        return pl.pallas_call(
            functools.partial(product_kernel, own_part, halves, resident),
            out_shape=[jax.ShapeDtypeStruct((out_rows, part), kind) for _ in halves],
            in_specs=[smem, smem, vmem if resident else hbm] + [anyw] * (2 + sum(2 + 2 * OVER_CUTS[h] for h in halves)),
            out_specs=[vmem] * len(halves),
            scratch_shapes=([] if resident else [pltpu.VMEM(held, jnp.bfloat16)])
            + [
                pltpu.VMEM((len(halves), SOURCES * rows + edge, part), jnp.bfloat16),
                pltpu.SemaphoreType.DMA((len(halves), 4 + max(OVER_CUTS))),
            ]
            + ([] if resident else [sems]),
            compiler_params=params if resident else wide,
            cost_estimate=TINY,
        )(index, spot2, tiles, *args)

    def rep_swap(x):
        return lax.ppermute(x, "rep", [(0, 1), (1, 0)])

    def base_of(features):
        return pl.pallas_call(
            base_kernel,
            out_shape=jax.ShapeDtypeStruct((out_rows, width), jnp.float32),
            in_specs=[smem, hbm, vmem, vmem],
            out_specs=vmem,
            scratch_shapes=[pltpu.VMEM((out_rows, width), jnp.bfloat16), pltpu.SemaphoreType.DMA],
            compiler_params=params,
            cost_estimate=TINY,
        )(spot, in_hbm(features), w_self, bias.reshape(1, width))

    def token_of(place):
        return pl.pallas_call(
            token_kernel,
            out_shape=jax.ShapeDtypeStruct((8, 128), jnp.int32),
            in_specs=[smem],
            out_specs=vmem,
            cost_estimate=pl.CostEstimate(flops=0, bytes_accessed=8 << 20, transcendentals=0),
        )(jnp.reshape(place, (1,)))

    takes_cross = (place % 4 == 1) | (place % 4 == 2)
    spot2 = jnp.stack([replica, takes_cross.astype(jnp.int32)])

    def halved(p, n):
        return [p[rows * q // n : rows * (q + 1) // n] for q in range(n)]

    (x0,), (x1,) = cross
    degree = degree_of(True, after(usable, spot2, index))
    degree_out, tiles_far = degree_of(False, after(usable, degree))
    base = base_of(after(features, degree))
    z0 = ahead_of(after(x0, degree_out, base))
    token = token_of(after(place, x1))
    z1 = ahead_of(x1)
    degree_far = rep_swap(degree_out)
    xo0 = [over(after(p, token)) for p in halved(x0, OVER_CUTS[0])]
    zo0 = [over(after(p, token)) for p in halved(z0, OVER_CUTS[0])]
    half0 = (x0, z0, *xo0, *zo0)
    (far0,) = product_of(False, (0,), tiles_far, after(features, degree_far), pair, *half0, resident=True)
    other0 = rep_swap(far0)
    xo1, zo1 = over(after(x1, far0)), over(after(z1, far0))
    half1 = (x1, z1, xo1, zo1)
    (far1,) = product_of(False, (1,), tiles_far, features, pair, *half1, resident=True)
    other1 = rep_swap(far1)
    nearby = product_of(True, (0, 1), adjacency, after(features, far1), pair, *half0, *half1)
    far = (other0, other1)

    return pl.pallas_call(
        final_kernel,
        out_shape=jax.ShapeDtypeStruct((out_rows, width), jnp.bfloat16),
        in_specs=[vmem] * 8,
        out_specs=vmem,
        compiler_params=params,
        cost_estimate=TINY,
    )(degree, degree_far, base, nearby[0], far[0], nearby[1], far[1], w_neigh)


def solution(mesh):
    placed = (P("row", None), P("row", "rep", None, None), P("row", "rep"), P("row"), P(), P(), P())
    return jax.shard_map(
        local, mesh=mesh, in_specs=placed, out_specs=P(("row", "rep"), None), check_vma=False
    )
```

```python
import functools

import jax
import jax.numpy as jnp
from jax import lax
from jax.experimental import pallas as pl
from jax.experimental.pallas import tpu as pltpu
from jax.sharding import PartitionSpec as P

OWN, PAIR, CROSS, AHEAD, LAST = range(5)
SOURCES = 5
HALVES = 2
CUTS = (2, 1)
GROUP = 2
VMEM_BYTES = 6 << 20
TINY = pl.CostEstimate(flops=0, bytes_accessed=0, transcendentals=0)


def after(x, *others):
    return lax.optimization_barrier((x, *others))[0]


def in_hbm(x):
    return pltpu.with_memory_space_constraint(x, pltpu.HBM)


def in_vmem(x):
    return pltpu.with_memory_space_constraint(x, pltpu.VMEM)


def swap_route(count, bit):
    return [(i, i ^ bit) for i in range(count)]


def loop_route(count):
    route = [(i, i + 4 if i % 4 < 2 else i - 4) for i in range(count)]
    return [(i, j if 0 <= j < count else i ^ 2) for i, j in route]


def ahead_route(count):
    return [(i, (i + 4) % count if i % 4 < 2 else (i - 4) % count) for i in range(count)]


def degree_kernel(own_part, usable, place, adj, degree, tiles, sems):
    rows = degree.shape[0]
    first = (place[0] if own_part else 1 - place[0]) * rows
    loads = [pltpu.make_async_copy(adj.at[first + i], tiles.at[i], sems.at[i]) for i in range(rows)]
    for load in loads:
        load.start()
    for i in range(rows):
        loads[i].wait()
        degree[i : i + 1, :] = degree_row(tiles, i, usable[first + i])


def degree_row(tiles, i, count):
    slots, edge = tiles.shape[1], tiles.shape[2]
    acc = jnp.zeros((edge, edge), jnp.float32)
    for s in range(slots):
        t = tiles[i, s]
        acc = acc + jnp.where(s < count, t, jnp.zeros_like(t)).astype(jnp.float32)
    return jnp.sum(acc.T, axis=0, keepdims=True)


def token_kernel(value, out):
    out[...] = jnp.full(out.shape, value[0], out.dtype)


def base_kernel(place, feats, w_self, bias, base, own, sem):
    half = own.shape[0]
    copy = pltpu.make_async_copy(feats.at[pl.ds(pl.multiple_of(place[0] * half, half), half)], own, sem)
    copy.start()
    copy.wait()
    base[...] = jnp.dot(own[...], w_self[...], preferred_element_type=jnp.float32) + bias[...]


def product_kernel(own_part, halves, resident, index, place, adj, feats, pair, *rest):
    counts = [4 * CUTS[h] for h in halves]
    pieces, rest = rest[: sum(counts)], rest[sum(counts) :]
    outs, rest = rest[: len(halves)], rest[len(halves) :]
    if resident:
        tiles = adj
        window, window_sems = rest
    else:
        tiles, window, window_sems, tile_sems = rest
    rows, slots, edge = tiles.shape[0], tiles.shape[1], tiles.shape[2]
    part = window.shape[2]
    shard = 2 * rows * edge
    first = (place[0] if own_part else 1 - place[0]) * rows

    copies, by_cross, by_ahead = [], [], []
    for k, h in enumerate(halves):

        def move(ref, at, m):
            return pltpu.make_async_copy(ref, window.at[k, pl.ds(at, ref.shape[0])], window_sems.at[k, m])

        columns = pl.ds(h * part, part)
        at, n = sum(counts[:k]), CUTS[h]
        cross, ahead, cross_over, ahead_over = (pieces[at + n * j : at + n * (j + 1)] for j in range(4))
        copies += [move(feats.at[:, columns], OWN * shard, 0), move(pair.at[:, columns], PAIR * shard, 1)]
        for q in range(n):
            row = 0 if n == 1 else (place[0] if q == 0 else 1 - place[0]) * (shard // n)
            copies += [move(cross[q], CROSS * shard + row, 2 + q), move(ahead[q], AHEAD * shard + row, 2 + n + q)]
            by_cross.append(move(cross_over[q], LAST * shard + row, 2 + 2 * n + q))
            by_ahead.append(move(ahead_over[q], LAST * shard + row, 2 + 2 * n + q))
    for copy in copies:
        copy.start()

    @pl.when(place[1] == 1)
    def _():
        for copy in by_cross:
            copy.start()

    @pl.when(place[1] == 0)
    def _():
        for copy in by_ahead:
            copy.start()

    if not resident:
        loads = [pltpu.make_async_copy(adj.at[first + i], tiles.at[i], tile_sems.at[i]) for i in range(rows)]
        for load in loads:
            load.start()
    for k in range(len(halves)):
        window[k, pl.ds(SOURCES * shard, edge), :] = jnp.zeros((edge, part), window.dtype)
    for copy in copies + by_cross:
        copy.wait()

    def block(at):
        cut = pl.ds(pl.multiple_of(at * edge, edge), edge)
        return jnp.concatenate([window[k, cut, :] for k in range(len(halves))], axis=1)

    for g in range(0, rows, GROUP):
        if not resident:
            for i in range(g, g + GROUP):
                loads[i].wait()
        for i in range(g, g + GROUP):
            acc = None
            for s in range(0, slots, 2):
                left = jnp.concatenate([tiles[i, s], tiles[i, s + 1]], axis=1)
                right = jnp.concatenate([block(index[first + i, s]), block(index[first + i, s + 1])], axis=0)
                d = jnp.dot(left, right, preferred_element_type=jnp.float32)
                acc = d if acc is None else acc + d
            for k, out in enumerate(outs):
                out[i * edge : (i + 1) * edge, :] = acc[:, k * part : (k + 1) * part].astype(out.dtype)


def final_kernel(degree, degree_far, base, own0, far0, own1, far1, w_neigh, out):
    rows, edge = degree.shape
    for i in range(rows):
        total = degree[i : i + 1, :] + degree_far[i : i + 1, :]
        scale = 1.0 / jnp.maximum(total, 1.0)
        column = jnp.broadcast_to(scale, (edge, edge)).T
        cut = pl.ds(i * edge, edge)
        mean = jnp.concatenate(
            [
                ((own0[cut, :] + far0[cut, :].astype(jnp.float32)) * column).astype(jnp.bfloat16),
                ((own1[cut, :] + far1[cut, :].astype(jnp.float32)) * column).astype(jnp.bfloat16),
            ],
            axis=1,
        )
        mixed = base[cut, :] + jnp.dot(mean, w_neigh[...], preferred_element_type=jnp.float32)
        out[cut, :] = jnp.maximum(mixed, 0.0).astype(out.dtype)


def local(features, adjacency, columns, live, w_self, w_neigh, bias):
    rows, width = features.shape
    block_rows, slots, edge, _ = adjacency.shape
    count = lax.axis_size("row")
    place = lax.axis_index("row")
    replica = lax.axis_index("rep")
    part = width // HALVES
    out_rows = rows // 2

    usable = jnp.clip(live - replica * slots, 0, slots)
    spot = jnp.reshape(replica, (1,)).astype(jnp.int32)

    offset = columns // block_rows - place
    to_pair = 1 - 2 * (place % 2)
    to_cross = jnp.where(place % 4 < 2, 2, -2)
    source = jnp.where(offset == to_pair, PAIR, jnp.where(offset == -to_pair, LAST, OWN))
    source = jnp.where(offset == to_cross, CROSS, jnp.where(offset == -to_cross, AHEAD, source))
    index = source * block_rows + columns % block_rows
    dead = jnp.arange(slots, dtype=jnp.int32)[None, :] >= usable[:, None]
    index = jnp.where(dead, SOURCES * block_rows, index).astype(jnp.int32)

    smem = pl.BlockSpec(memory_space=pltpu.SMEM)
    vmem = pl.BlockSpec(memory_space=pltpu.VMEM)
    hbm = pl.BlockSpec(memory_space=pltpu.HBM)
    params = pltpu.CompilerParams(vmem_limit_bytes=VMEM_BYTES)

    def cross_of(sent):
        return lax.ppermute(sent, "row", swap_route(count, 2))

    x0a = cross_of(lax.dynamic_slice(features, (replica * out_rows, 0), (out_rows, part)))
    x1 = cross_of(features[:, part:])
    pair = lax.ppermute(features, "row", swap_route(count, 1))

    wide = pltpu.CompilerParams(vmem_limit_bytes=16 << 20)
    anyw = pl.BlockSpec(memory_space=pl.ANY)
    adjacency = in_hbm(adjacency)

    def ahead_of(p):
        return lax.ppermute(p, "row", ahead_route(count))

    def over(p):
        return lax.ppermute(p, "row", swap_route(count, 1))

    held = (block_rows // 2, slots, edge, edge)
    sems = pltpu.SemaphoreType.DMA((block_rows // 2,))

    def degree_of(own_part, usable):
        shape = jax.ShapeDtypeStruct((block_rows // 2, edge), jnp.float32)
        tiles = pltpu.VMEM(held, jnp.bfloat16)
        outs = pl.pallas_call(
            functools.partial(degree_kernel, own_part),
            out_shape=[shape] if own_part else [shape, tiles],
            in_specs=[smem, smem, hbm],
            out_specs=[vmem] if own_part else [vmem, vmem],
            scratch_shapes=[tiles, sems] if own_part else [sems],
            compiler_params=wide if own_part else params,
            cost_estimate=TINY,
        )(usable, spot, adjacency)
        return outs[0] if own_part else (outs[0], in_vmem(outs[1]))

    def product_of(own_part, halves, tiles, *args, resident=False):
        kind = jnp.float32 if own_part else jnp.bfloat16
        return pl.pallas_call(
            functools.partial(product_kernel, own_part, halves, resident),
            out_shape=[jax.ShapeDtypeStruct((out_rows, part), kind) for _ in halves],
            in_specs=[smem, smem, vmem if resident else hbm] + [anyw] * (2 + sum(4 * CUTS[h] for h in halves)),
            out_specs=[vmem] * len(halves),
            scratch_shapes=([] if resident else [pltpu.VMEM(held, jnp.bfloat16)])
            + [
                pltpu.VMEM((len(halves), SOURCES * rows + edge, part), jnp.bfloat16),
                pltpu.SemaphoreType.DMA((len(halves), 2 + 3 * max(CUTS))),
            ]
            + ([] if resident else [sems]),
            compiler_params=params if resident else wide,
            cost_estimate=TINY,
        )(index, spot2, tiles, *args)

    def rep_swap(x):
        return lax.ppermute(x, "rep", [(0, 1), (1, 0)])

    def base_of(features):
        return pl.pallas_call(
            base_kernel,
            out_shape=jax.ShapeDtypeStruct((out_rows, width), jnp.float32),
            in_specs=[smem, hbm, vmem, vmem],
            out_specs=vmem,
            scratch_shapes=[pltpu.VMEM((out_rows, width), jnp.bfloat16), pltpu.SemaphoreType.DMA],
            compiler_params=params,
            cost_estimate=TINY,
        )(spot, in_hbm(features), w_self, bias.reshape(1, width))

    def token_of(place):
        return pl.pallas_call(
            token_kernel,
            out_shape=jax.ShapeDtypeStruct((8, 128), jnp.int32),
            in_specs=[smem],
            out_specs=vmem,
            cost_estimate=pl.CostEstimate(flops=0, bytes_accessed=8 << 20, transcendentals=0),
        )(jnp.reshape(place, (1,)))

    takes_cross = (place % 4 == 1) | (place % 4 == 2)
    spot2 = jnp.stack([replica, takes_cross.astype(jnp.int32)])

    degree = degree_of(True, after(usable, spot2, index))
    z0a, x0b, xo0a = ahead_of(after(x0a, degree)), rep_swap(after(x0a, degree)), over(after(x0a, degree))
    degree_out, tiles_far = degree_of(False, after(usable, xo0a))
    z0b = rep_swap(after(z0a, degree_out))
    base = base_of(after(features, degree_out))
    z1 = lax.ppermute(after(x1, base), "row", loop_route(count))
    degree_far = rep_swap(degree_out)
    xo0, zo0 = (xo0a, over(after(x0b, x1))), (over(after(z0a, x1)), over(after(z0b, x1)))
    half0 = (x0a, x0b, z0a, z0b, *xo0, *zo0)
    (far0,) = product_of(False, (0,), tiles_far, after(features, degree_far), pair, *half0, resident=True)
    other0 = rep_swap(far0)
    xo1, zo1 = over(after(x1, far0)), over(after(z1, far0))
    half1 = (x1, z1, xo1, zo1)
    (far1,) = product_of(False, (1,), tiles_far, features, pair, *half1, resident=True)
    other1 = rep_swap(far1)
    nearby = product_of(True, (0, 1), adjacency, after(features, far1), pair, *half0, *half1)
    far = (other0, other1)

    return pl.pallas_call(
        final_kernel,
        out_shape=jax.ShapeDtypeStruct((out_rows, width), jnp.bfloat16),
        in_specs=[vmem] * 8,
        out_specs=vmem,
        compiler_params=params,
        cost_estimate=TINY,
    )(degree, degree_far, base, nearby[0], far[0], nearby[1], far[1], w_neigh)


def solution(mesh):
    placed = (P("row", None), P("row", "rep", None, None), P("row", "rep"), P("row"), P(), P(), P())
    return jax.shard_map(
        local, mesh=mesh, in_specs=placed, out_specs=P(("row", "rep"), None), check_vma=False
    )
```

```python
import functools

import jax
import jax.numpy as jnp
from jax import lax
from jax.experimental import pallas as pl
from jax.experimental.pallas import tpu as pltpu
from jax.sharding import PartitionSpec as P

OWN, PAIR, CROSS, AHEAD, LAST = range(5)
SOURCES = 5
HALVES = 2
OVER = (0, 3, 6, 8)
ARGS = (8, 6)
GROUP = 2
VMEM_BYTES = 6 << 20
TINY = pl.CostEstimate(flops=0, bytes_accessed=0, transcendentals=0)


def after(x, *others):
    return lax.optimization_barrier((x, *others))[0]


def in_hbm(x):
    return pltpu.with_memory_space_constraint(x, pltpu.HBM)


def in_vmem(x):
    return pltpu.with_memory_space_constraint(x, pltpu.VMEM)


def swap_route(count, bit):
    return [(i, i ^ bit) for i in range(count)]


def loop_route(count):
    route = [(i, i + 4 if i % 4 < 2 else i - 4) for i in range(count)]
    return [(i, j if 0 <= j < count else i ^ 2) for i, j in route]


def ahead_route(count):
    return [(i, (i + 4) % count if i % 4 < 2 else (i - 4) % count) for i in range(count)]


def degree_kernel(own_part, usable, place, adj, degree, tiles, sems):
    rows = degree.shape[0]
    first = (place[0] if own_part else 1 - place[0]) * rows
    loads = [pltpu.make_async_copy(adj.at[first + i], tiles.at[i], sems.at[i]) for i in range(rows)]
    for load in loads:
        load.start()
    for i in range(rows):
        loads[i].wait()
        degree[i : i + 1, :] = degree_row(tiles, i, usable[first + i])


def degree_row(tiles, i, count):
    slots, edge = tiles.shape[1], tiles.shape[2]
    acc = jnp.zeros((edge, edge), jnp.float32)
    for s in range(slots):
        t = tiles[i, s]
        acc = acc + jnp.where(s < count, t, jnp.zeros_like(t)).astype(jnp.float32)
    return jnp.sum(acc.T, axis=0, keepdims=True)


def token_kernel(value, out):
    out[...] = jnp.full(out.shape, value[0], out.dtype)


def base_kernel(place, feats, w_self, bias, base, own, sem):
    half = own.shape[0]
    copy = pltpu.make_async_copy(feats.at[pl.ds(pl.multiple_of(place[0] * half, half), half)], own, sem)
    copy.start()
    copy.wait()
    base[...] = jnp.dot(own[...], w_self[...], preferred_element_type=jnp.float32) + bias[...]


def product_kernel(own_part, halves, resident, index, place, adj, feats, pair, *rest):
    count = sum(ARGS[h] for h in halves)
    pieces, rest = rest[:count], rest[count:]
    outs, rest = rest[: len(halves)], rest[len(halves) :]
    if resident:
        tiles = adj
        window, window_sems = rest
    else:
        tiles, window, window_sems, tile_sems = rest
    rows, slots, edge = tiles.shape[0], tiles.shape[1], tiles.shape[2]
    part = window.shape[2]
    shard = 2 * rows * edge
    first = (place[0] if own_part else 1 - place[0]) * rows

    copies, by_cross, by_ahead = [], [], []
    for k, h in enumerate(halves):

        def move(ref, at, m):
            return pltpu.make_async_copy(ref, window.at[k, pl.ds(at, ref.shape[0])], window_sems.at[k, m])

        columns = pl.ds(h * part, part)
        mine, pieces = pieces[: ARGS[h]], pieces[ARGS[h] :]
        copies += [move(feats.at[:, columns], OWN * shard, 0), move(pair.at[:, columns], PAIR * shard, 1)]
        if h == 0:
            starts = over_starts = [place[0] * (shard // 2), (1 - place[0]) * (shard // 2)]
        else:
            starts, over_starts = [0], [shard * e // 8 for e in OVER[:-1]]
        n, m = len(starts), len(over_starts)
        cross, ahead, cross_over, ahead_over = mine[:n], mine[n : 2 * n], mine[2 * n : 3 * n], mine[3 * n :]
        for q in range(n):
            copies += [move(cross[q], CROSS * shard + starts[q], 2 + q), move(ahead[q], AHEAD * shard + starts[q], 4 + q)]
            by_cross.append(move(cross_over[q], LAST * shard + starts[q], 6 + q))
        by_ahead += [move(ahead_over[q], LAST * shard + over_starts[q], 6 + q) for q in range(m)]
    for copy in copies:
        copy.start()

    sources = ((1, by_cross), (0, by_ahead))
    for flag, some in sources:

        @pl.when(place[1] == flag)
        def _(some=some):
            for copy in some:
                copy.start()

    if not resident:
        loads = [pltpu.make_async_copy(adj.at[first + i], tiles.at[i], tile_sems.at[i]) for i in range(rows)]
        for load in loads:
            load.start()
    for k in range(len(halves)):
        window[k, pl.ds(SOURCES * shard, edge), :] = jnp.zeros((edge, part), window.dtype)
    for copy in copies:
        copy.wait()
    for flag, some in sources:

        @pl.when(place[1] == flag)
        def _(some=some):
            for copy in some:
                copy.wait()

    def block(at):
        cut = pl.ds(pl.multiple_of(at * edge, edge), edge)
        return jnp.concatenate([window[k, cut, :] for k in range(len(halves))], axis=1)

    for g in range(0, rows, GROUP):
        if not resident:
            for i in range(g, g + GROUP):
                loads[i].wait()
        for i in range(g, g + GROUP):
            acc = None
            for s in range(0, slots, 2):
                left = jnp.concatenate([tiles[i, s], tiles[i, s + 1]], axis=1)
                right = jnp.concatenate([block(index[first + i, s]), block(index[first + i, s + 1])], axis=0)
                d = jnp.dot(left, right, preferred_element_type=jnp.float32)
                acc = d if acc is None else acc + d
            for k, out in enumerate(outs):
                out[i * edge : (i + 1) * edge, :] = acc[:, k * part : (k + 1) * part].astype(out.dtype)


def final_kernel(degree, degree_far, base, own0, far0, own1, far1, w_neigh, out):
    rows, edge = degree.shape
    for i in range(rows):
        total = degree[i : i + 1, :] + degree_far[i : i + 1, :]
        scale = 1.0 / jnp.maximum(total, 1.0)
        column = jnp.broadcast_to(scale, (edge, edge)).T
        cut = pl.ds(i * edge, edge)
        mean = jnp.concatenate(
            [
                ((own0[cut, :] + far0[cut, :].astype(jnp.float32)) * column).astype(jnp.bfloat16),
                ((own1[cut, :] + far1[cut, :].astype(jnp.float32)) * column).astype(jnp.bfloat16),
            ],
            axis=1,
        )
        mixed = base[cut, :] + jnp.dot(mean, w_neigh[...], preferred_element_type=jnp.float32)
        out[cut, :] = jnp.maximum(mixed, 0.0).astype(out.dtype)


def local(features, adjacency, columns, live, w_self, w_neigh, bias):
    rows, width = features.shape
    block_rows, slots, edge, _ = adjacency.shape
    count = lax.axis_size("row")
    place = lax.axis_index("row")
    replica = lax.axis_index("rep")
    part = width // HALVES
    out_rows = rows // 2

    usable = jnp.clip(live - replica * slots, 0, slots)
    spot = jnp.reshape(replica, (1,)).astype(jnp.int32)

    offset = columns // block_rows - place
    to_pair = 1 - 2 * (place % 2)
    to_cross = jnp.where(place % 4 < 2, 2, -2)
    source = jnp.where(offset == to_pair, PAIR, jnp.where(offset == -to_pair, LAST, OWN))
    source = jnp.where(offset == to_cross, CROSS, jnp.where(offset == -to_cross, AHEAD, source))
    index = source * block_rows + columns % block_rows
    dead = jnp.arange(slots, dtype=jnp.int32)[None, :] >= usable[:, None]
    index = jnp.where(dead, SOURCES * block_rows, index).astype(jnp.int32)

    smem = pl.BlockSpec(memory_space=pltpu.SMEM)
    vmem = pl.BlockSpec(memory_space=pltpu.VMEM)
    hbm = pl.BlockSpec(memory_space=pltpu.HBM)
    params = pltpu.CompilerParams(vmem_limit_bytes=VMEM_BYTES)

    def cross_of(sent):
        return lax.ppermute(sent, "row", swap_route(count, 2))

    x0a = cross_of(lax.dynamic_slice(features, (replica * out_rows, 0), (out_rows, part)))
    x1 = cross_of(features[:, part:])
    pair = lax.ppermute(features, "row", swap_route(count, 1))

    wide = pltpu.CompilerParams(vmem_limit_bytes=16 << 20)
    anyw = pl.BlockSpec(memory_space=pl.ANY)
    adjacency = in_hbm(adjacency)

    def ahead_of(p):
        return lax.ppermute(p, "row", ahead_route(count))

    def over(p):
        return lax.ppermute(p, "row", swap_route(count, 1))

    held = (block_rows // 2, slots, edge, edge)
    sems = pltpu.SemaphoreType.DMA((block_rows // 2,))

    def degree_of(own_part, usable):
        shape = jax.ShapeDtypeStruct((block_rows // 2, edge), jnp.float32)
        tiles = pltpu.VMEM(held, jnp.bfloat16)
        outs = pl.pallas_call(
            functools.partial(degree_kernel, own_part),
            out_shape=[shape] if own_part else [shape, tiles],
            in_specs=[smem, smem, hbm],
            out_specs=[vmem] if own_part else [vmem, vmem],
            scratch_shapes=[tiles, sems] if own_part else [sems],
            compiler_params=wide if own_part else params,
            cost_estimate=TINY,
        )(usable, spot, adjacency)
        return outs[0] if own_part else (outs[0], in_vmem(outs[1]))

    def product_of(own_part, halves, tiles, *args, resident=False):
        kind = jnp.float32 if own_part else jnp.bfloat16
        return pl.pallas_call(
            functools.partial(product_kernel, own_part, halves, resident),
            out_shape=[jax.ShapeDtypeStruct((out_rows, part), kind) for _ in halves],
            in_specs=[smem, smem, vmem if resident else hbm] + [anyw] * (2 + sum(ARGS[h] for h in halves)),
            out_specs=[vmem] * len(halves),
            scratch_shapes=([] if resident else [pltpu.VMEM(held, jnp.bfloat16)])
            + [
                pltpu.VMEM((len(halves), SOURCES * rows + edge, part), jnp.bfloat16),
                pltpu.SemaphoreType.DMA((len(halves), 6 + len(OVER))),
            ]
            + ([] if resident else [sems]),
            compiler_params=params if resident else wide,
            cost_estimate=TINY,
        )(index, spot2, tiles, *args)

    def rep_swap(x):
        return lax.ppermute(x, "rep", [(0, 1), (1, 0)])

    def base_of(features):
        return pl.pallas_call(
            base_kernel,
            out_shape=jax.ShapeDtypeStruct((out_rows, width), jnp.float32),
            in_specs=[smem, hbm, vmem, vmem],
            out_specs=vmem,
            scratch_shapes=[pltpu.VMEM((out_rows, width), jnp.bfloat16), pltpu.SemaphoreType.DMA],
            compiler_params=params,
            cost_estimate=TINY,
        )(spot, in_hbm(features), w_self, bias.reshape(1, width))

    def token_of(place):
        return pl.pallas_call(
            token_kernel,
            out_shape=jax.ShapeDtypeStruct((8, 128), jnp.int32),
            in_specs=[smem],
            out_specs=vmem,
            cost_estimate=pl.CostEstimate(flops=0, bytes_accessed=8 << 20, transcendentals=0),
        )(jnp.reshape(place, (1,)))

    takes_cross = (place % 4 == 1) | (place % 4 == 2)
    spot2 = jnp.stack([replica, takes_cross.astype(jnp.int32)])

    def loop_of(p):
        return lax.ppermute(p, "row", loop_route(count))

    degree = degree_of(True, usable)
    z0a, x0b, xo0a = ahead_of(after(x0a, degree)), rep_swap(after(x0a, degree)), over(after(x0a, degree))
    degree_out, tiles_far = degree_of(False, after(usable, xo0a, index, spot2))
    z0b = rep_swap(after(z0a, degree_out))
    base = base_of(after(features, degree_out))
    z1 = loop_of(after(x1, base))
    degree_far = rep_swap(degree_out)
    xo0, zo0 = (xo0a, over(after(x0b, x1))), (over(after(z0a, x1)), over(after(z0b, x1)))
    half0 = (x0a, x0b, z0a, z0b, *xo0, *zo0)
    (far0,) = product_of(False, (0,), tiles_far, after(features, degree_far), pair, *half0, resident=True)
    other0 = rep_swap(far0)
    xo1 = over(after(x1, far0))
    cuts = [rows * e // 8 for e in OVER]
    zo1 = [over(after(z1, far0)[start:stop]) for start, stop in zip(cuts, cuts[1:])]
    half1 = (x1, z1, xo1, *zo1)
    (far1,) = product_of(False, (1,), tiles_far, features, pair, *half1, resident=True)
    other1 = rep_swap(after(far1, other0))
    nearby = product_of(True, (0, 1), adjacency, after(features, far1), pair, *half0, *half1)
    far = (other0, other1)

    return pl.pallas_call(
        final_kernel,
        out_shape=jax.ShapeDtypeStruct((out_rows, width), jnp.bfloat16),
        in_specs=[vmem] * 8,
        out_specs=vmem,
        compiler_params=params,
        cost_estimate=TINY,
    )(degree, degree_far, base, nearby[0], far[0], nearby[1], far[1], w_neigh)


def solution(mesh):
    placed = (P("row", None), P("row", "rep", None, None), P("row", "rep"), P("row"), P(), P(), P())
    return jax.shard_map(
        local, mesh=mesh, in_specs=placed, out_specs=P(("row", "rep"), None), check_vma=False
    )
```

```python
import functools

import jax
import jax.numpy as jnp
from jax import lax
from jax.experimental import pallas as pl
from jax.experimental.pallas import tpu as pltpu
from jax.sharding import PartitionSpec as P

OWN, PAIR, CROSS, AHEAD, LAST = range(5)
SOURCES = 5
HALVES = 2
OVER = (0, 3, 6, 8)
ARGS = (8, 6)
GROUP = 2
VMEM_BYTES = 6 << 20
TINY = pl.CostEstimate(flops=0, bytes_accessed=0, transcendentals=0)


def after(x, *others):
    return lax.optimization_barrier((x, *others))[0]


def in_hbm(x):
    return pltpu.with_memory_space_constraint(x, pltpu.HBM)


def in_vmem(x):
    return pltpu.with_memory_space_constraint(x, pltpu.VMEM)


def swap_route(count, bit):
    return [(i, i ^ bit) for i in range(count)]


def loop_route(count):
    route = [(i, i + 4 if i % 4 < 2 else i - 4) for i in range(count)]
    return [(i, j if 0 <= j < count else i ^ 2) for i, j in route]


def ahead_route(count):
    return [(i, (i + 4) % count if i % 4 < 2 else (i - 4) % count) for i in range(count)]


def degree_kernel(own_part, usable, place, adj, degree, tiles, sems):
    rows = degree.shape[0]
    first = (place[0] if own_part else 1 - place[0]) * rows
    loads = [pltpu.make_async_copy(adj.at[first + i], tiles.at[i], sems.at[i]) for i in range(rows)]
    for load in loads:
        load.start()
    for i in range(rows):
        loads[i].wait()
        degree[i : i + 1, :] = degree_row(tiles, i, usable[first + i])


def degree_row(tiles, i, count):
    slots, edge = tiles.shape[1], tiles.shape[2]
    acc = jnp.zeros((edge, edge), jnp.float32)
    for s in range(slots):
        t = tiles[i, s]
        acc = acc + jnp.where(s < count, t, jnp.zeros_like(t)).astype(jnp.float32)
    return jnp.sum(acc.T, axis=0, keepdims=True)


def token_kernel(value, out):
    out[...] = jnp.full(out.shape, value[0], out.dtype)


def base_kernel(place, feats, w_self, bias, base, own, sem):
    half = own.shape[0]
    copy = pltpu.make_async_copy(feats.at[pl.ds(pl.multiple_of(place[0] * half, half), half)], own, sem)
    copy.start()
    copy.wait()
    base[...] = jnp.dot(own[...], w_self[...], preferred_element_type=jnp.float32) + bias[...]


def product_kernel(own_part, halves, resident, index, place, adj, feats, pair, *rest):
    count = sum(ARGS[h] for h in halves)
    pieces, rest = rest[:count], rest[count:]
    outs, rest = rest[: len(halves)], rest[len(halves) :]
    if resident:
        tiles = adj
        window, window_sems = rest
    else:
        tiles, window, window_sems, tile_sems = rest
    rows, slots, edge = tiles.shape[0], tiles.shape[1], tiles.shape[2]
    part = window.shape[2]
    shard = 2 * rows * edge
    first = (place[0] if own_part else 1 - place[0]) * rows

    copies, by_cross, by_ahead = [], [], []
    for k, h in enumerate(halves):

        def move(ref, at, m):
            return pltpu.make_async_copy(ref, window.at[k, pl.ds(at, ref.shape[0])], window_sems.at[k, m])

        columns = pl.ds(h * part, part)
        mine, pieces = pieces[: ARGS[h]], pieces[ARGS[h] :]
        copies += [move(feats.at[:, columns], OWN * shard, 0), move(pair.at[:, columns], PAIR * shard, 1)]
        if h == 0:
            starts = over_starts = [place[0] * (shard // 2), (1 - place[0]) * (shard // 2)]
        else:
            starts, over_starts = [0], [shard * e // 8 for e in OVER[:-1]]
        n, m = len(starts), len(over_starts)
        cross, ahead, cross_over, ahead_over = mine[:n], mine[n : 2 * n], mine[2 * n : 3 * n], mine[3 * n :]
        for q in range(n):
            copies += [move(cross[q], CROSS * shard + starts[q], 2 + q), move(ahead[q], AHEAD * shard + starts[q], 4 + q)]
            by_cross.append(move(cross_over[q], LAST * shard + starts[q], 6 + q))
        by_ahead += [move(ahead_over[q], LAST * shard + over_starts[q], 6 + q) for q in range(m)]
    for copy in copies:
        copy.start()

    sources = ((1, by_cross), (0, by_ahead))
    for flag, some in sources:

        @pl.when(place[1] == flag)
        def _(some=some):
            for copy in some:
                copy.start()

    if not resident:
        loads = [pltpu.make_async_copy(adj.at[first + i], tiles.at[i], tile_sems.at[i]) for i in range(rows)]
        for load in loads:
            load.start()
    for k in range(len(halves)):
        window[k, pl.ds(SOURCES * shard, edge), :] = jnp.zeros((edge, part), window.dtype)
    for copy in copies:
        copy.wait()
    for flag, some in sources:

        @pl.when(place[1] == flag)
        def _(some=some):
            for copy in some:
                copy.wait()

    def block(at):
        cut = pl.ds(pl.multiple_of(at * edge, edge), edge)
        return jnp.concatenate([window[k, cut, :] for k in range(len(halves))], axis=1)

    for g in range(0, rows, GROUP):
        if not resident:
            for i in range(g, g + GROUP):
                loads[i].wait()
        for i in range(g, g + GROUP):
            acc = None
            for s in range(0, slots, 2):
                left = jnp.concatenate([tiles[i, s], tiles[i, s + 1]], axis=1)
                right = jnp.concatenate([block(index[first + i, s]), block(index[first + i, s + 1])], axis=0)
                d = jnp.dot(left, right, preferred_element_type=jnp.float32)
                acc = d if acc is None else acc + d
            for k, out in enumerate(outs):
                out[i * edge : (i + 1) * edge, :] = acc[:, k * part : (k + 1) * part].astype(out.dtype)


def middle_kernel(degree, degree_far, base, own0, far0, w_neigh, mixed, column):
    rows, edge = degree.shape
    part = own0.shape[1]
    for i in range(rows):
        total = degree[i : i + 1, :] + degree_far[i : i + 1, :]
        scale = 1.0 / jnp.maximum(total, 1.0)
        cut = pl.ds(i * edge, edge)
        column[cut, :] = jnp.broadcast_to(scale, (edge, edge)).T
        mean = ((own0[cut, :] + far0[cut, :].astype(jnp.float32)) * column[cut, :]).astype(jnp.bfloat16)
        mixed[cut, :] = base[cut, :] + jnp.dot(mean, w_neigh[:part, :], preferred_element_type=jnp.float32)


def final_kernel(column, mixed, own1, far1, w_neigh, out):
    edge = column.shape[1]
    part = own1.shape[1]
    for i in range(column.shape[0] // edge):
        cut = pl.ds(i * edge, edge)
        mean = ((own1[cut, :] + far1[cut, :].astype(jnp.float32)) * column[cut, :]).astype(jnp.bfloat16)
        total = mixed[cut, :] + jnp.dot(mean, w_neigh[part:, :], preferred_element_type=jnp.float32)
        out[cut, :] = jnp.maximum(total, 0.0).astype(out.dtype)


def local(features, adjacency, columns, live, w_self, w_neigh, bias):
    rows, width = features.shape
    block_rows, slots, edge, _ = adjacency.shape
    count = lax.axis_size("row")
    place = lax.axis_index("row")
    replica = lax.axis_index("rep")
    part = width // HALVES
    out_rows = rows // 2

    usable = jnp.clip(live - replica * slots, 0, slots)
    spot = jnp.reshape(replica, (1,)).astype(jnp.int32)

    offset = columns // block_rows - place
    to_pair = 1 - 2 * (place % 2)
    to_cross = jnp.where(place % 4 < 2, 2, -2)
    source = jnp.where(offset == to_pair, PAIR, jnp.where(offset == -to_pair, LAST, OWN))
    source = jnp.where(offset == to_cross, CROSS, jnp.where(offset == -to_cross, AHEAD, source))
    index = source * block_rows + columns % block_rows
    dead = jnp.arange(slots, dtype=jnp.int32)[None, :] >= usable[:, None]
    index = jnp.where(dead, SOURCES * block_rows, index).astype(jnp.int32)

    smem = pl.BlockSpec(memory_space=pltpu.SMEM)
    vmem = pl.BlockSpec(memory_space=pltpu.VMEM)
    hbm = pl.BlockSpec(memory_space=pltpu.HBM)
    params = pltpu.CompilerParams(vmem_limit_bytes=VMEM_BYTES)

    def cross_of(sent):
        return lax.ppermute(sent, "row", swap_route(count, 2))

    x0a = cross_of(lax.dynamic_slice(features, (replica * out_rows, 0), (out_rows, part)))
    x1 = cross_of(features[:, part:])
    pair = lax.ppermute(features, "row", swap_route(count, 1))

    wide = pltpu.CompilerParams(vmem_limit_bytes=16 << 20)
    anyw = pl.BlockSpec(memory_space=pl.ANY)
    adjacency = in_hbm(adjacency)

    def ahead_of(p):
        return lax.ppermute(p, "row", ahead_route(count))

    def over(p):
        return lax.ppermute(p, "row", swap_route(count, 1))

    held = (block_rows // 2, slots, edge, edge)
    sems = pltpu.SemaphoreType.DMA((block_rows // 2,))

    def degree_of(own_part, usable):
        shape = jax.ShapeDtypeStruct((block_rows // 2, edge), jnp.float32)
        tiles = pltpu.VMEM(held, jnp.bfloat16)
        outs = pl.pallas_call(
            functools.partial(degree_kernel, own_part),
            out_shape=[shape] if own_part else [shape, tiles],
            in_specs=[smem, smem, hbm],
            out_specs=[vmem] if own_part else [vmem, vmem],
            scratch_shapes=[tiles, sems] if own_part else [sems],
            compiler_params=wide if own_part else params,
            cost_estimate=TINY,
        )(usable, spot, adjacency)
        return outs[0] if own_part else (outs[0], in_vmem(outs[1]))

    def product_of(own_part, halves, tiles, *args, resident=False):
        kind = jnp.float32 if own_part else jnp.bfloat16
        return pl.pallas_call(
            functools.partial(product_kernel, own_part, halves, resident),
            out_shape=[jax.ShapeDtypeStruct((out_rows, part), kind) for _ in halves],
            in_specs=[smem, smem, vmem if resident else hbm] + [anyw] * (2 + sum(ARGS[h] for h in halves)),
            out_specs=[vmem] * len(halves),
            scratch_shapes=([] if resident else [pltpu.VMEM(held, jnp.bfloat16)])
            + [
                pltpu.VMEM((len(halves), SOURCES * rows + edge, part), jnp.bfloat16),
                pltpu.SemaphoreType.DMA((len(halves), 6 + len(OVER))),
            ]
            + ([] if resident else [sems]),
            compiler_params=params if resident else wide,
            cost_estimate=TINY,
        )(index, spot2, tiles, *args)

    def rep_swap(x):
        return lax.ppermute(x, "rep", [(0, 1), (1, 0)])

    def base_of(features):
        return pl.pallas_call(
            base_kernel,
            out_shape=jax.ShapeDtypeStruct((out_rows, width), jnp.float32),
            in_specs=[smem, hbm, vmem, vmem],
            out_specs=vmem,
            scratch_shapes=[pltpu.VMEM((out_rows, width), jnp.bfloat16), pltpu.SemaphoreType.DMA],
            compiler_params=params,
            cost_estimate=TINY,
        )(spot, in_hbm(features), w_self, bias.reshape(1, width))

    def token_of(place):
        return pl.pallas_call(
            token_kernel,
            out_shape=jax.ShapeDtypeStruct((8, 128), jnp.int32),
            in_specs=[smem],
            out_specs=vmem,
            cost_estimate=pl.CostEstimate(flops=0, bytes_accessed=8 << 20, transcendentals=0),
        )(jnp.reshape(place, (1,)))

    takes_cross = (place % 4 == 1) | (place % 4 == 2)
    spot2 = jnp.stack([replica, takes_cross.astype(jnp.int32)])

    def loop_of(p):
        return lax.ppermute(p, "row", loop_route(count))

    degree = degree_of(True, usable)
    z0a, x0b, xo0a = ahead_of(after(x0a, degree)), rep_swap(after(x0a, degree)), over(after(x0a, degree))
    degree_out, tiles_far = degree_of(False, after(usable, xo0a, index, spot2))
    z0b = rep_swap(after(z0a, degree_out))
    base = base_of(after(features, degree_out))
    z1 = loop_of(after(x1, base))
    degree_far = rep_swap(degree_out)
    xo0, zo0 = (xo0a, over(after(x0b, x1))), (over(after(z0a, x1)), over(after(z0b, x1)))
    half0 = (x0a, x0b, z0a, z0b, *xo0, *zo0)
    (far0,) = product_of(False, (0,), tiles_far, after(features, degree_far), pair, *half0, resident=True)
    other0 = rep_swap(far0)
    xo1 = over(after(x1, far0))
    cuts = [rows * e // 8 for e in OVER]
    zo1 = [over(after(z1, far0)[start:stop]) for start, stop in zip(cuts, cuts[1:])]
    half1 = (x1, z1, xo1, *zo1)
    (far1,) = product_of(False, (1,), tiles_far, features, pair, *half1, resident=True)
    other1 = rep_swap(after(far1, other0))
    nearby = product_of(True, (0, 1), adjacency, after(features, far1), pair, *half0, *half1)
    far = (other0, other1)

    mixed, column = pl.pallas_call(
        middle_kernel,
        out_shape=[jax.ShapeDtypeStruct((out_rows, n), jnp.float32) for n in (width, edge)],
        in_specs=[vmem] * 6,
        out_specs=[vmem] * 2,
        compiler_params=params,
        cost_estimate=TINY,
    )(degree, degree_far, base, nearby[0], far[0], w_neigh)
    return pl.pallas_call(
        final_kernel,
        out_shape=jax.ShapeDtypeStruct((out_rows, width), jnp.bfloat16),
        in_specs=[vmem] * 5,
        out_specs=vmem,
        compiler_params=params,
        cost_estimate=TINY,
    )(column, mixed, nearby[1], far[1], w_neigh)


def solution(mesh):
    placed = (P("row", None), P("row", "rep", None, None), P("row", "rep"), P("row"), P(), P(), P())
    return jax.shard_map(
        local, mesh=mesh, in_specs=placed, out_specs=P(("row", "rep"), None), check_vma=False
    )
```
